128 devices in a mesh: dp: 16 (over z, y), tensor: 8 (over x, core).
Axes of the slice: x: 4, y: 4, z: 4, core: 2. Of those that a mesh axis runs over, the one named last changes fastest.
Arguments:
- tokens: bfloat16 [6144, 6144], P('dp'), may hold values from -6 to 6
- grad_out: bfloat16 [6144, 6144], P('dp'), may hold values from -6 to 6
- gate_weight: bfloat16 [96, 12, 128, 128], P('tensor'), may hold values from -0.15625 to 0.15625
- up_weight: bfloat16 [96, 12, 128, 128], P('tensor'), may hold values from -0.15625 to 0.15625
- down_weight: bfloat16 [96, 12, 128, 128], P('tensor'), may hold values from -0.109375 to 0.109375
- gate_index: int32 [96, 12], P('tensor'), may hold values from 0 to 47, as said below
- up_index: int32 [96, 12], P('tensor'), may hold values from 0 to 47, as said below
- down_index: int32 [96, 12], P('tensor'), may hold values from 0 to 47, as said below
Outputs:
- input_grad: bfloat16 [6144, 6144], P(('dp', 'tensor'))
- grad_gate: float32 [96, 1536, 128], P('tensor', 'dp')
- grad_up: float32 [96, 1536, 128], P('tensor', 'dp')
- grad_down: float32 [96, 1536, 128], P('tensor', 'dp')
The draws below stay inside these ranges and needn't reach their ends.
Inputs may be any that keep to these rules, and one draw needn't show every extreme that they name: `gate_index`: each row holds 12 different block numbers. `up_index`: each row holds 12 different block numbers. `down_index`: each row holds 12 different block numbers.
All inputs are finite; a program needn't handle non-finite values.
Results may differ from the reference program's by a relative error of at most 0.02.
Values may be sent and summed in bfloat16 or wider, within the bound.
No kernel may reach another device: no remote copies, remote signals or barrier semaphores. Data moves between devices by JAX's collectives and lax.ppermute only.
A program may use at most 256 MiB of HBM per device.

```python
import math
import jax
import jax.numpy as jnp
from jax import lax

BLOCK = 128
D = 6144
TOK_DEV = 384
DB = 48
HB = 96
HL = 12
NNZ = 12
TOKENS = 6144
N_DP = 16
N_TENSOR = 8


def pick_blocks(key):
    row_keys = jax.random.split(key, HB)

    def one_row(row_key):
        return jax.random.permutation(row_key, DB)[:NNZ]
    return jax.vmap(one_row)(row_keys).astype(jnp.int32)


def draw_gate_index(key, part):
    key = jax.random.fold_in(key, 11)
    return pick_blocks(key)


def draw_up_index(key, part):
    key = jax.random.fold_in(key, 23)
    return pick_blocks(key)


def draw_down_index(key, part):
    key = jax.random.fold_in(key, 37)
    return pick_blocks(key)


def shard_levels(own_key, shape, pieces, low, top_value):
    def one(axis_at, shards_of):
        draws = jax.random.uniform(jax.random.fold_in(jax.random.fold_in(own_key, 6), axis_at), (shards_of,), jnp.float32, low / len(pieces), top_value / len(pieces))
        return jnp.repeat(jnp.exp(draws), shape[axis_at] // shards_of).reshape((-1,) + (1,) * (len(shape) - axis_at - 1))

    factor_of = one(*pieces[0])
    for cut in pieces[1:]:
        factor_of = factor_of * one(*cut)
    return factor_of


def bell_draw(key, dims, spread, most, cuts=(), held_as=jnp.bfloat16):
    result = jax.random.normal(key, dims, jnp.float32) * spread
    if len(cuts) > 0:
        result = shard_levels(key, dims, cuts, -0.22, 0.18) * result
    return jnp.clip(result, min=-most, max=most).astype(held_as)


def setup_inputs(seed: int = 0) -> dict:
    key_of = jax.random.split(jax.random.key(seed), 9)
    tokens = bell_draw(key_of[0], (TOKENS, D), 1.0, 6.0, ((0, 16),))
    grad_out = bell_draw(key_of[1], (TOKENS, D), 1.0, 6.0, ((0, 16),))
    gate_weight = bell_draw(key_of[2], (HB, NNZ, BLOCK, BLOCK), (NNZ * BLOCK) ** -0.5, 0.15625, ((0, 8),))
    up_weight = bell_draw(key_of[3], (HB, NNZ, BLOCK, BLOCK), (NNZ * BLOCK) ** -0.5, 0.15625, ((0, 8),))
    down_weight = bell_draw(key_of[4], (HB, NNZ, BLOCK, BLOCK), (HB * NNZ * BLOCK // DB) ** -0.5, 0.109375, ((0, 8),))
    gate_index = draw_gate_index(jax.random.fold_in(key_of[8], 71), 0)
    up_index = draw_up_index(jax.random.fold_in(key_of[8], 71), 0)
    down_index = draw_down_index(jax.random.fold_in(key_of[8], 71), 0)
    return dict(tokens=tokens, grad_out=grad_out, gate_weight=gate_weight, up_weight=up_weight, down_weight=down_weight, gate_index=gate_index, up_index=up_index, down_index=down_index)


PRECISE = lax.Precision.HIGHEST

def rounded(values):
    return lax.optimization_barrier(values.astype(jnp.bfloat16)).astype(jnp.float32)

def take_blocks(activations, block_ids):
    shaped = activations.reshape(activations.shape[0], DB, BLOCK)
    return jnp.take(shaped, block_ids, axis=1)

def reference(tokens, grad_out, gate_weight, up_weight, down_weight, gate_index, up_index, down_index):
    grad_scale = 1.0 / math.sqrt(TOKENS)

    def shard_pass(carried, shard):
        first_block = (shard * HL).astype(jnp.int32)
        w_gate = lax.dynamic_slice_in_dim(gate_weight, first_block, HL, 0).astype(jnp.float32)
        w_up = lax.dynamic_slice_in_dim(up_weight, first_block, HL, 0).astype(jnp.float32)
        w_down = lax.dynamic_slice_in_dim(down_weight, first_block, HL, 0).astype(jnp.float32)
        ids_gate = lax.dynamic_slice_in_dim(gate_index, first_block, HL, 0).astype(jnp.int32)
        ids_up = lax.dynamic_slice_in_dim(up_index, first_block, HL, 0).astype(jnp.int32)
        ids_down = lax.dynamic_slice_in_dim(down_index, first_block, HL, 0).astype(jnp.int32)

        def group_pass(sums, group):
            first_row = (group * TOK_DEV).astype(jnp.int32)
            tok_rows = lax.dynamic_slice_in_dim(tokens, first_row, TOK_DEV, 0).astype(jnp.float32)
            out_rows = lax.dynamic_slice_in_dim(grad_out, first_row, TOK_DEV, 0).astype(jnp.float32)
            tok_gate = take_blocks(tok_rows, ids_gate)
            tok_up = take_blocks(tok_rows, ids_up)
            out_down = take_blocks(out_rows, ids_down)
            gate_lin = jnp.einsum('tjkd,jkdf->tjf', tok_gate, w_gate, precision=PRECISE)
            up_lin = jnp.einsum('tjkd,jkdf->tjf', tok_up, w_up, precision=PRECISE)
            hidden_grad = jnp.einsum('tjke,jkfe->tjf', out_down, w_down, precision=PRECISE)
            sigmoid_gate = jax.nn.sigmoid(gate_lin)
            activated = gate_lin * sigmoid_gate
            hidden = rounded(activated * up_lin)
            up_grad = rounded(hidden_grad * activated)
            gate_grad = rounded(hidden_grad * up_lin * sigmoid_gate * (1.0 + gate_lin * (1.0 - sigmoid_gate)))
            down_term = rounded(jnp.einsum('tjf,tjke->jkfe', hidden, out_down, precision=PRECISE) * grad_scale)
            gate_term = rounded(jnp.einsum('tjkd,tjf->jkdf', tok_gate, gate_grad, precision=PRECISE) * grad_scale)
            up_term = rounded(jnp.einsum('tjkd,tjf->jkdf', tok_up, up_grad, precision=PRECISE) * grad_scale)
            back_gate = jnp.einsum('tjf,jkdf->tjkd', gate_grad, w_gate, precision=PRECISE)
            back_up = jnp.einsum('tjf,jkdf->tjkd', up_grad, w_up, precision=PRECISE)
            placed = jnp.zeros((TOK_DEV, DB, BLOCK), jnp.float32)
            placed = placed.at[:, ids_gate.reshape(-1)].add(back_gate.reshape(TOK_DEV, HL * NNZ, BLOCK))
            placed = placed.at[:, ids_up.reshape(-1)].add(back_up.reshape(TOK_DEV, HL * NNZ, BLOCK))
            partial_rows = lax.optimization_barrier(placed.reshape(TOK_DEV, D).astype(jnp.bfloat16))
            return ((sums[0] + gate_term, sums[1] + up_term, sums[2] + down_term), partial_rows)
        zero_grad = jnp.zeros((HL, NNZ, BLOCK, BLOCK), jnp.float32)
        sums, partials = lax.scan(group_pass, (zero_grad, zero_grad, zero_grad), jnp.arange(N_DP, dtype=jnp.int32))
        return (carried + partials.astype(jnp.float32).reshape(TOKENS, D), sums)
    input_sum, grads = lax.scan(shard_pass, jnp.zeros((TOKENS, D), jnp.float32), jnp.arange(N_TENSOR, dtype=jnp.int32))
    grad_gate = grads[0].reshape(HB, NNZ * BLOCK, BLOCK)
    grad_up = grads[1].reshape(HB, NNZ * BLOCK, BLOCK)
    grad_down = grads[2].reshape(HB, NNZ * BLOCK, BLOCK)
    return (input_sum.astype(jnp.bfloat16), grad_gate, grad_up, grad_down)
```

```python
import functools
import math

import jax
import jax.numpy as jnp
from jax import lax
from jax.experimental import pallas as pl
from jax.experimental.pallas import tpu as pltpu
from jax.sharding import PartitionSpec as P

BLK = 128
ROWS = 96
SET = 3 * ROWS
NNZ = 12
BF = jnp.bfloat16
F32 = jnp.float32
CHUNKS = (7,5)
VMEM_BYTES = 53 << 20
FULL_BYTES = 63 << 20
LONG = 200 * 10**9


def dot(a, b):
    return jnp.dot(a, b, preferred_element_type=F32)


def dot_nt(a, b):
    return lax.dot_general(a, b, (((1,), (1,)), ((), ())), preferred_element_type=F32)


def dot_tn(a, b):
    return lax.dot_general(a, b, (((0,), (0,)), ((), ())), preferred_element_type=F32)


def block_at(ref, block):
    return ref[:, pl.ds(pl.multiple_of(block * BLK, BLK), BLK)]


def chunk_kernel(
    first, scale,
    gate_ids, up_ids, down_ids, place,
    tok, out_grad, w_gate, w_up, w_down, *rest,
):
    far_p, far_m, plus, minus, own, gate_out, up_out, terms = rest[-8:]
    step = pl.program_id(0)
    j = first + step
    y, z, flip = place[0], place[1], place[2]

    def forward(source, ids, weight, transposed):
        half = source.shape[0] // 2
        return jnp.concatenate(
            [forward_rows(source, ids, weight, transposed, r, half) for r in (0, half)], axis=0
        )

    def forward_rows(source, ids, weight, transposed, row, rows):
        total = None
        for k in range(0, NNZ, 2):
            left = jnp.concatenate(
                [block_at(source, ids[j, k + i])[row : row + rows] for i in range(2)], axis=1
            )
            if transposed:
                right = jnp.concatenate([weight[0, k], weight[0, k + 1]], axis=1)
                part = dot_nt(left, right)
            else:
                part = dot(left, weight[0, k : k + 2].reshape(2 * BLK, BLK))
            total = part if total is None else total + part
        return total

    gate_lin = forward(tok, gate_ids, w_gate, False)
    up_lin = forward(tok, up_ids, w_up, False)

    hidden_grad = forward(out_grad, down_ids, w_down, True)
    sigmoid = jax.nn.sigmoid(gate_lin)
    activated = gate_lin * sigmoid
    hidden = (activated * up_lin).astype(BF)
    up_grad = (hidden_grad * activated).astype(BF)
    gate_grad = (
        hidden_grad * up_lin * sigmoid * (1.0 + gate_lin * (1.0 - sigmoid))
    ).astype(BF)
    gate_out[...] = gate_grad
    up_out[...] = up_grad
    hidden_t = hidden.T

    def put(z_rel, w, term):
        for shard in range(4):
            y_rel = lax.rem(shard - y + 4, 4)
            at = jnp.where(flip == 0, y_rel * 4 + z_rel, z_rel * 4 + y_rel)
            terms[at, w * ROWS : (w + 1) * ROWS] = term[shard * ROWS : (shard + 1) * ROWS]

    for z_rel in range(4):
        group = 3 * lax.rem(z + z_rel, 4)
        for w, (ids, grad) in enumerate(((gate_ids, gate_grad), (up_ids, up_grad))):
            left = jnp.concatenate([block_at(tok, ids[j, group + i]) for i in range(3)], axis=1)
            put(z_rel, w, (dot_tn(left, grad) * scale).astype(BF))
        right = jnp.concatenate(
            [block_at(out_grad, down_ids[j, group + i]) for i in range(3)], axis=1
        )
        wide = (dot(hidden_t, right) * scale).astype(BF)
        put(z_rel, 2, jnp.concatenate([wide[:, i * BLK : (i + 1) * BLK] for i in range(3)], axis=0))

    own[...] = terms[0:4]
    plus[...] = terms[4:8]
    far_p[...] = terms[8:10]
    far_m[...] = terms[10:12]
    minus[...] = terms[12:16]


def run_chunk(first, size, scale, ids, place, tok, out_grad, weights, grads, after):
    tokens = tok.shape[0]
    hbm = pl.BlockSpec(memory_space=pl.ANY)
    vmem = pl.BlockSpec(memory_space=pltpu.VMEM)
    weight = pl.BlockSpec((1, NNZ, BLK, BLK), lambda i, *_: (first + i, 0, 0, 0))
    hidden = pl.BlockSpec((tokens, BLK), lambda i, *_: (0, first + i))
    extra = [*(grads or ()), *after]

    def terms_of(n):
        return pl.BlockSpec((n, SET, BLK), lambda i, *_: (0, i, 0)), jax.ShapeDtypeStruct(
            (n, size * SET, BLK), BF
        )

    far, direct = terms_of(2), terms_of(4)
    grad_shape = jax.ShapeDtypeStruct((tokens, weights[0].shape[0] * BLK), BF)
    return pl.pallas_call(
        functools.partial(chunk_kernel, first, scale),
        grid_spec=pltpu.PrefetchScalarGridSpec(
            num_scalar_prefetch=4,
            grid=(size,),
            in_specs=[vmem] * 2 + [weight] * 3 + [hbm] * len(extra),
            out_specs=[far[0]] * 2 + [direct[0]] * 3 + [hidden] * 2,
            scratch_shapes=[pltpu.VMEM((16, SET, BLK), BF)],
        ),
        out_shape=[far[1]] * 2 + [direct[1]] * 3 + [grad_shape] * 2,
        input_output_aliases={9: 5, 10: 6} if grads else {},
        compiler_params=pltpu.CompilerParams(vmem_limit_bytes=VMEM_BYTES),
        cost_estimate=pl.CostEstimate(
            flops=size * NNZ * 12 * tokens * BLK * BLK, bytes_accessed=20 << 20, transcendentals=0
        ),
        name="chunk",
    )(*ids, place, tok, out_grad, *weights, *extra)


def back_kernel(gate_ids, up_ids, gate_grad, up_grad, w_gate, w_up, out, token, total, piece, sem):
    j = pl.program_id(0)
    rows, width = total.shape

    @pl.when(j == 0)
    def _():
        total[...] = jnp.zeros_like(total)
        token[...] = jnp.zeros_like(token)

    for ids, grad, weight in ((gate_ids, gate_grad, w_gate), (up_ids, up_grad, w_up)):
        for k in range(0, NNZ, 2):
            right = weight[0, k : k + 2].reshape(2 * BLK, BLK)
            part = jnp.concatenate(
                [dot_nt(grad[r : r + rows // 2], right) for r in (0, rows // 2)], axis=0
            )
            for i in range(2):
                at = pl.ds(pl.multiple_of(ids[j, k + i] * BLK, BLK), BLK)
                total[:, at] = total[:, at] + part[:, i * BLK : (i + 1) * BLK]

    @pl.when(j == pl.num_programs(0) - 1)
    def _():
        count = 4
        step = width // count
        copies = []
        for q in range(count):
            at = pl.ds(q * step, step)
            piece[q] = total[:, at].astype(BF)
            copies.append(pltpu.make_async_copy(piece.at[q], out.at[:, at], sem.at[q]))
            copies[-1].start()
        for copy in copies:
            copy.wait()


def run_back(ids, gate_grad, up_grad, w_gate, w_up, width, after):
    tokens = gate_grad.shape[0]
    blocks = w_gate.shape[0]
    hidden = pl.BlockSpec((tokens, BLK), lambda i, *_: (0, i))
    weight = pl.BlockSpec((1, NNZ, BLK, BLK), lambda i, *_: (i, 0, 0, 0))
    hbm = pl.BlockSpec(memory_space=pl.ANY)

    def kernel(*refs):
        back_kernel(*refs[:6], *refs[6 + len(after) :])

    return pl.pallas_call(
        kernel,
        grid_spec=pltpu.PrefetchScalarGridSpec(
            num_scalar_prefetch=2,
            grid=(blocks,),
            in_specs=[hidden, hidden, weight, weight] + [hbm] * len(after),
            out_specs=[hbm, pl.BlockSpec((8, BLK), lambda i, *_: (0, 0))],
            scratch_shapes=[
                pltpu.VMEM((tokens, width), F32),
                pltpu.VMEM((4, tokens, width // 4), BF),
                pltpu.SemaphoreType.DMA((4,)),
            ],
        ),
        out_shape=[
            jax.ShapeDtypeStruct((tokens, width), BF),
            jax.ShapeDtypeStruct((8, BLK), F32),
        ],
        compiler_params=pltpu.CompilerParams(vmem_limit_bytes=FULL_BYTES),
        cost_estimate=pl.CostEstimate(
            flops=blocks * NNZ * 4 * tokens * BLK * BLK, bytes_accessed=16 << 20, transcendentals=0
        ),
        name="back",
    )(*ids, gate_grad, up_grad, w_gate, w_up, *after)


def wide(a):
    return a[...].astype(F32)


def call(kernel, name, grid, in_specs, out_specs, out_shape, args, aliases=None, after=(), room=False, flops=0):
    taken = len(args)

    def run(*refs):
        kernel(*refs[:taken], *refs[taken + len(after) :])

    return pl.pallas_call(
        run,
        grid=grid,
        in_specs=in_specs + [pl.BlockSpec(memory_space=pl.ANY)] * len(after),
        out_specs=out_specs,
        out_shape=out_shape,
        input_output_aliases=aliases or {},
        compiler_params=pltpu.CompilerParams(vmem_limit_bytes=VMEM_BYTES if room else FULL_BYTES),
        cost_estimate=pl.CostEstimate(flops=flops, bytes_accessed=0, transcendentals=0),
        name=name,
    )(*args, *after)


def far_kernel(far_p, far_m, plus, minus, plus_out, minus_out):
    plus_out[...] = (wide(plus) + wide(far_p)).astype(BF)
    minus_out[...] = (wide(minus) + wide(far_m)).astype(BF)


def add_far(far_p, far_m, plus, minus, **order):
    rows = plus.shape[1]
    one = (1, rows, BLK)
    low = pl.BlockSpec(one, lambda i: (i, 0, 0))
    high = pl.BlockSpec(one, lambda i: (i + 2, 0, 0))
    shape = jax.ShapeDtypeStruct(plus.shape, BF)
    return call(
        far_kernel, "add_far", (2,), [low, low, low, high], [low, high], [shape, shape],
        (far_p, far_m, plus, minus), {2: 0, 3: 1}, **order,
    )


def near_kernel(own, got_p, got_m, far_p, far_m, plus, minus, kept):
    total = (wide(own) + wide(got_p) + wide(got_m)).astype(BF)
    kept[...] = total[0]
    plus[...] = total[1]
    minus[...] = total[3]

    @pl.when(pl.program_id(0) == 0)
    def _():
        far_p[...] = total[2]

    @pl.when(pl.program_id(0) == 1)
    def _():
        far_m[...] = total[2]


def add_near(own, got_p, got_m, **order):
    half = own.shape[1] // 2
    block = pl.BlockSpec((4, half, BLK), lambda i: (0, i, 0))
    part = pl.BlockSpec((half, BLK), lambda i: (i, 0))
    fixed = pl.BlockSpec((half, BLK), lambda i: (0, 0))
    small = jax.ShapeDtypeStruct((half, BLK), BF)
    large = jax.ShapeDtypeStruct((2 * half, BLK), BF)
    return call(
        near_kernel, "add_near", (2,), [block] * 3, [fixed] * 2 + [part] * 3,
        [small] * 2 + [large] * 3, (own, got_p, got_m), **order,
    )


def add_far2(far_p, far_m, plus, minus, **order):
    half = far_p.shape[0]
    whole = pl.BlockSpec((half, BLK), lambda i: (0, 0))
    high = pl.BlockSpec((half, BLK), lambda i: (1, 0))
    shape = jax.ShapeDtypeStruct(plus.shape, BF)
    return call(
        far_kernel, "add_far2", (1,), [whole, whole, whole, high], [whole, high], [shape, shape],
        (far_p, far_m, plus, minus), {2: 0, 3: 1}, **order,
    )


def last_kernel(size, kept, got_p, got_m, *outs):
    total = wide(kept) + wide(got_p) + wide(got_m)
    for i in range(size):
        for w in range(3):
            outs[w - 3][i] = total[i * SET + w * ROWS : i * SET + (w + 1) * ROWS]


def add_last(first, size, blocks, kept, got_p, got_m, grads, flops=0):
    whole = pl.BlockSpec(kept.shape, lambda i: (0, 0))
    step = math.gcd(first, size) if first else size
    hbm = pl.BlockSpec(memory_space=pl.ANY)
    spec = pl.BlockSpec((step, ROWS, BLK), lambda i: (first // step + i, 0, 0))
    part = pl.BlockSpec((step * SET, BLK), lambda i: (i, 0))
    shape = jax.ShapeDtypeStruct((blocks, ROWS, BLK), F32)
    given = [] if grads is None else list(grads)
    return call(
        functools.partial(last_kernel, step), "add_last", (size // step,),
        [part] * 3 + [hbm] * len(given), [spec] * 3, [shape] * 3,
        (kept, got_p, got_m, *given), {3 + i: i for i in range(len(given))}, flops=flops,
    )


def body(tokens, grad_out, gate_weight, up_weight, down_weight, gate_index, up_index, down_index):
    row_count, width = tokens.shape
    scale = 1.0 / math.sqrt(row_count * lax.axis_size("dp"))
    me, flip = lax.axis_index("dp"), lax.rem(lax.axis_index("tensor"), 2)
    place = jnp.stack([lax.rem(me, 4), lax.div(me, 4), flip]).astype(jnp.int32)
    ids = (gate_index, up_index, down_index)
    weights = (gate_weight, up_weight, down_weight)
    blocks = gate_weight.shape[0]

    def pairs(second, by):
        found = []
        for z in range(4):
            for y in range(4):
                for t in range(8):
                    along_y = (t % 2 == 0) != second
                    to = (z, (y + by) % 4) if along_y else ((z + by) % 4, y)
                    found.append(((z * 4 + y) * 8 + t, (to[0] * 4 + to[1]) * 8 + t))
        return found

    def send(up, down, second):
        axes = ("dp", "tensor")
        return (
            lax.ppermute(up, axes, pairs(second, 1)),
            lax.ppermute(down, axes, pairs(second, -1)),
        )

    starts = [sum(CHUNKS[:c]) for c in range(len(CHUNKS))]
    made, sent, grads = [], {}, None

    def chunk(c, *after):
        made.append(
            run_chunk(
                starts[c], CHUNKS[c], scale, ids, place, tokens, grad_out, weights,
                made[-1][5:] if made else None, after,
            )
        )

    def far(c, **order):
        far_p, far_m, plus, minus = made[c][:4]
        sent[c] = add_far(*send(far_p, far_m, False), plus, minus, **order)

    def near(c, **order):
        sent[c] = add_near(made[c][4], *send(*sent[c], False), **order)

    def far2(c, **order):
        far_p, far_m, plus, minus, kept = sent[c]
        sent[c] = (*add_far2(*send(far_p, far_m, True), plus, minus, **order), kept)

    def last(c, grads, flops=0):
        plus, minus, kept = sent[c]
        return add_last(starts[c], CHUNKS[c], blocks, kept, *send(plus, minus, True), grads, flops)

    chunk(0)
    chunk(1)
    far(0, after=(made[1][0],))
    partial, token = run_back(
        ids[:2], *made[1][5:], gate_weight, up_weight, width, (sent[0][0],)
    )
    summed = lax.psum_scatter(partial, "tensor", scatter_dimension=0, tiled=True)
    far(1, after=(token,), flops=LONG)
    near(0, after=(sent[1][0],))
    far2(0)
    near(1, after=(sent[0][0],))
    grads = last(0, grads)
    far2(1)
    grads = last(1, grads)
    return (summed, *grads)


def solution(mesh):
    in_specs = (
        P("dp", None),
        P("dp", None),
        P("tensor", None, None, None),
        P("tensor", None, None, None),
        P("tensor", None, None, None),
        P("tensor", None),
        P("tensor", None),
        P("tensor", None),
    )
    out_specs = (
        P(("dp", "tensor"), None),
        P("tensor", "dp", None),
        P("tensor", "dp", None),
        P("tensor", "dp", None),
    )
    return jax.shard_map(body, mesh=mesh, in_specs=in_specs, out_specs=out_specs, check_vma=False)
```

```python
import functools
import math

import jax
import jax.numpy as jnp
from jax import lax
from jax.experimental import pallas as pl
from jax.experimental.pallas import tpu as pltpu
from jax.sharding import PartitionSpec as P

BLK = 128
ROWS = 96
SET = 3 * ROWS
NNZ = 12
BF = jnp.bfloat16
F32 = jnp.float32
CHUNKS = (7,5)
VMEM_BYTES = 53 << 20
FULL_BYTES = (64 << 20) - (64 << 10)
LONG = 200 * 10**9


def dot(a, b):
    return jnp.dot(a, b, preferred_element_type=F32)


def dot_nt(a, b):
    return lax.dot_general(a, b, (((1,), (1,)), ((), ())), preferred_element_type=F32)


def block_at(ref, block):
    return ref[:, pl.ds(pl.multiple_of(block * BLK, BLK), BLK)]


def chunk_kernel(
    first, scale,
    gate_ids, up_ids, down_ids, place,
    tok, out_grad, w_gate, w_up, w_down, *rest,
):
    far_p, far_m, plus, minus, own, gate_out, up_out, terms = rest[-8:]
    step = pl.program_id(0)
    j = first + step
    y, z, flip = place[0], place[1], place[2]

    def forward(source, ids, weight, transposed):
        half = source.shape[0] // 2
        return jnp.concatenate(
            [forward_rows(source, ids, weight, transposed, r, half) for r in (0, half)], axis=0
        )

    def forward_rows(source, ids, weight, transposed, row, rows):
        total = None
        for k in range(0, NNZ, 2):
            left = jnp.concatenate(
                [block_at(source, ids[j, k + i])[row : row + rows] for i in range(2)], axis=1
            )
            if transposed:
                right = jnp.concatenate([weight[0, k], weight[0, k + 1]], axis=1)
                part = dot_nt(left, right)
            else:
                part = dot(left, weight[0, k : k + 2].reshape(2 * BLK, BLK))
            total = part if total is None else total + part
        return total

    gate_lin = forward(tok, gate_ids, w_gate, False)
    up_lin = forward(tok, up_ids, w_up, False)

    hidden_grad = forward(out_grad, down_ids, w_down, True)
    sigmoid = jax.nn.sigmoid(gate_lin)
    activated = gate_lin * sigmoid
    hidden = (activated * up_lin).astype(BF)
    up_grad = (hidden_grad * activated).astype(BF)
    gate_grad = (
        hidden_grad * up_lin * sigmoid * (1.0 + gate_lin * (1.0 - sigmoid))
    ).astype(BF)
    gate_out[...] = gate_grad
    up_out[...] = up_grad
    hidden_t, gate_t, up_t = hidden.T, gate_grad.T, up_grad.T

    def put(z_rel, w, term):
        for shard in range(4):
            y_rel = lax.rem(shard - y + 4, 4)
            at = jnp.where(flip == 0, y_rel * 4 + z_rel, z_rel * 4 + y_rel)
            terms[at, w * ROWS : (w + 1) * ROWS] = term[shard * ROWS : (shard + 1) * ROWS]

    for z_rel in range(4):
        group = 3 * lax.rem(z + z_rel, 4)
        wide = []
        for left, source, ids in (
            (gate_t, tok, gate_ids), (up_t, tok, up_ids), (hidden_t, out_grad, down_ids)
        ):
            right = jnp.concatenate(
                [block_at(source, ids[j, group + i]) for i in range(3)], axis=1
            )
            wide.append((dot(left, right) * scale).astype(BF))
        for w, term in enumerate(wide):
            parts = [term[:, i * BLK : (i + 1) * BLK] for i in range(3)]
            put(z_rel, w, jnp.concatenate(parts if w == 2 else [p.T for p in parts], axis=0))

    own[...] = terms[0:4]
    plus[...] = terms[4:8]
    far_p[...] = terms[8:10]
    far_m[...] = terms[10:12]
    minus[...] = terms[12:16]


def run_chunk(first, size, scale, ids, place, tok, out_grad, weights, grads, after):
    tokens = tok.shape[0]
    hbm = pl.BlockSpec(memory_space=pl.ANY)
    vmem = pl.BlockSpec(memory_space=pltpu.VMEM)
    weight = pl.BlockSpec((1, NNZ, BLK, BLK), lambda i, *_: (first + i, 0, 0, 0))
    hidden = pl.BlockSpec((tokens, BLK), lambda i, *_: (0, first + i))
    extra = [*(grads or ()), *after]

    def terms_of(n):
        return pl.BlockSpec((n, SET, BLK), lambda i, *_: (0, i, 0)), jax.ShapeDtypeStruct(
            (n, size * SET, BLK), BF
        )

    far, direct = terms_of(2), terms_of(4)
    grad_shape = jax.ShapeDtypeStruct((tokens, weights[0].shape[0] * BLK), BF)
    return pl.pallas_call(
        functools.partial(chunk_kernel, first, scale),
        grid_spec=pltpu.PrefetchScalarGridSpec(
            num_scalar_prefetch=4,
            grid=(size,),
            in_specs=[vmem] * 2 + [weight] * 3 + [hbm] * len(extra),
            out_specs=[far[0]] * 2 + [direct[0]] * 3 + [hidden] * 2,
            scratch_shapes=[pltpu.VMEM((16, SET, BLK), BF)],
        ),
        out_shape=[far[1]] * 2 + [direct[1]] * 3 + [grad_shape] * 2,
        input_output_aliases={9: 5, 10: 6} if grads else {},
        compiler_params=pltpu.CompilerParams(vmem_limit_bytes=VMEM_BYTES),
        cost_estimate=pl.CostEstimate(
            flops=25 * 10**9, bytes_accessed=20 << 20, transcendentals=0
        ),
        name="chunk",
    )(*ids, place, tok, out_grad, *weights, *extra)


def back_kernel(gate_ids, up_ids, gate_grad, up_grad, w_gate, w_up, out, token, total, piece, sem):
    j = pl.program_id(0)
    rows, width = total.shape

    @pl.when(j == 0)
    def _():
        total[...] = jnp.zeros_like(total)
        token[...] = jnp.zeros_like(token)

    for ids, grad, weight in ((gate_ids, gate_grad, w_gate), (up_ids, up_grad, w_up)):
        for k in range(0, NNZ, 2):
            right = weight[0, k : k + 2].reshape(2 * BLK, BLK)
            part = jnp.concatenate(
                [dot_nt(grad[r : r + rows // 2], right) for r in (0, rows // 2)], axis=0
            )
            for i in range(2):
                at = pl.ds(pl.multiple_of(ids[j, k + i] * BLK, BLK), BLK)
                total[:, at] = total[:, at] + part[:, i * BLK : (i + 1) * BLK]

    @pl.when(j == pl.num_programs(0) - 1)
    def _():
        count = 4
        step = width // count
        copies = []
        for q in range(count):
            at = pl.ds(q * step, step)
            piece[q] = total[:, at].astype(BF)
            copies.append(pltpu.make_async_copy(piece.at[q], out.at[:, at], sem.at[q]))
            copies[-1].start()
        for copy in copies:
            copy.wait()


def run_back(ids, gate_grad, up_grad, w_gate, w_up, width, after):
    tokens = gate_grad.shape[0]
    blocks = w_gate.shape[0]
    hidden = pl.BlockSpec((tokens, BLK), lambda i, *_: (0, i))
    weight = pl.BlockSpec((1, NNZ, BLK, BLK), lambda i, *_: (i, 0, 0, 0))
    hbm = pl.BlockSpec(memory_space=pl.ANY)

    def kernel(*refs):
        back_kernel(*refs[:6], *refs[6 + len(after) :])

    return pl.pallas_call(
        kernel,
        grid_spec=pltpu.PrefetchScalarGridSpec(
            num_scalar_prefetch=2,
            grid=(blocks,),
            in_specs=[hidden, hidden, weight, weight] + [hbm] * len(after),
            out_specs=[hbm, pl.BlockSpec((8, BLK), lambda i, *_: (0, 0))],
            scratch_shapes=[
                pltpu.VMEM((tokens, width), F32),
                pltpu.VMEM((4, tokens, width // 4), BF),
                pltpu.SemaphoreType.DMA((4,)),
            ],
        ),
        out_shape=[
            jax.ShapeDtypeStruct((tokens, width), BF),
            jax.ShapeDtypeStruct((8, BLK), F32),
        ],
        compiler_params=pltpu.CompilerParams(vmem_limit_bytes=FULL_BYTES),
        cost_estimate=pl.CostEstimate(
            flops=25 * 10**9, bytes_accessed=16 << 20, transcendentals=0
        ),
        name="back",
    )(*ids, gate_grad, up_grad, w_gate, w_up, *after)


def wide(a):
    return a[...].astype(F32)


def call(kernel, name, grid, in_specs, out_specs, out_shape, args, aliases=None, after=(), room=False, flops=0):
    taken = len(args)

    def run(*refs):
        kernel(*refs[:taken], *refs[taken + len(after) :])

    return pl.pallas_call(
        run,
        grid=grid,
        in_specs=in_specs + [pl.BlockSpec(memory_space=pl.ANY)] * len(after),
        out_specs=out_specs,
        out_shape=out_shape,
        input_output_aliases=aliases or {},
        compiler_params=pltpu.CompilerParams(vmem_limit_bytes=VMEM_BYTES if room else FULL_BYTES),
        cost_estimate=pl.CostEstimate(flops=flops, bytes_accessed=0, transcendentals=0),
        name=name,
    )(*args, *after)


def far_kernel(far_p, far_m, plus, minus, plus_out, minus_out):
    plus_out[...] = (wide(plus) + wide(far_p)).astype(BF)
    minus_out[...] = (wide(minus) + wide(far_m)).astype(BF)


def add_far(far_p, far_m, plus, minus, **order):
    rows = plus.shape[1]
    one = (1, rows, BLK)
    low = pl.BlockSpec(one, lambda i: (i, 0, 0))
    high = pl.BlockSpec(one, lambda i: (i + 2, 0, 0))
    shape = jax.ShapeDtypeStruct(plus.shape, BF)
    return call(
        far_kernel, "add_far", (2,), [low, low, low, high], [low, high], [shape, shape],
        (far_p, far_m, plus, minus), {2: 0, 3: 1}, **order,
    )


def near_kernel(own, got_p, got_m, far_p, far_m, plus, minus, kept):
    total = (wide(own) + wide(got_p) + wide(got_m)).astype(BF)
    kept[...] = total[0]
    plus[...] = total[1]
    minus[...] = total[3]

    @pl.when(pl.program_id(0) == 0)
    def _():
        far_p[...] = total[2]

    @pl.when(pl.program_id(0) == 1)
    def _():
        far_m[...] = total[2]


def add_near(own, got_p, got_m, **order):
    half = own.shape[1] // 2
    block = pl.BlockSpec((4, half, BLK), lambda i: (0, i, 0))
    part = pl.BlockSpec((half, BLK), lambda i: (i, 0))
    fixed = pl.BlockSpec((half, BLK), lambda i: (0, 0))
    small = jax.ShapeDtypeStruct((half, BLK), BF)
    large = jax.ShapeDtypeStruct((2 * half, BLK), BF)
    return call(
        near_kernel, "add_near", (2,), [block] * 3, [fixed] * 2 + [part] * 3,
        [small] * 2 + [large] * 3, (own, got_p, got_m), **order,
    )


def add_far2(far_p, far_m, plus, minus, **order):
    half = far_p.shape[0]
    whole = pl.BlockSpec((half, BLK), lambda i: (0, 0))
    high = pl.BlockSpec((half, BLK), lambda i: (1, 0))
    shape = jax.ShapeDtypeStruct(plus.shape, BF)
    return call(
        far_kernel, "add_far2", (1,), [whole, whole, whole, high], [whole, high], [shape, shape],
        (far_p, far_m, plus, minus), {2: 0, 3: 1}, **order,
    )


def last_kernel(first, size, kept, got_p, got_m, *refs):
    outs, total, sem = refs[-5:-2], refs[-2], refs[-1]
    sums = wide(kept) + wide(got_p) + wide(got_m)
    copies = []
    for w in range(3):
        for i in range(size):
            total[w, i] = sums[i * SET + w * ROWS : i * SET + (w + 1) * ROWS]
        to = outs[w].at[pl.ds(first, size)]
        copies.append(pltpu.make_async_copy(total.at[w], to, sem.at[w]))
        copies[-1].start()
    for copy in copies:
        copy.wait()


def add_last(first, size, blocks, kept, got_p, got_m, grads):
    whole = pl.BlockSpec(kept.shape, lambda i: (0, 0))
    hbm = pl.BlockSpec(memory_space=pl.ANY)
    given = [] if grads is None else list(grads)
    return pl.pallas_call(
        functools.partial(last_kernel, first, size),
        grid=(1,),
        in_specs=[whole] * 3 + [hbm] * len(given),
        out_specs=[hbm] * 3,
        out_shape=[jax.ShapeDtypeStruct((blocks, ROWS, BLK), F32)] * 3,
        scratch_shapes=[
            pltpu.VMEM((3, size, ROWS, BLK), F32),
            pltpu.SemaphoreType.DMA((3,)),
        ],
        input_output_aliases={3 + i: i for i in range(len(given))},
        compiler_params=pltpu.CompilerParams(vmem_limit_bytes=FULL_BYTES),
        cost_estimate=pl.CostEstimate(flops=0, bytes_accessed=0, transcendentals=0),
        name="add_last",
    )(kept, got_p, got_m, *given)


def body(tokens, grad_out, gate_weight, up_weight, down_weight, gate_index, up_index, down_index):
    row_count, width = tokens.shape
    scale = 1.0 / math.sqrt(row_count * lax.axis_size("dp"))
    me, flip = lax.axis_index("dp"), lax.rem(lax.axis_index("tensor"), 2)
    places = [
        jnp.stack([lax.rem(me, 4), lax.div(me, 4), flip]).astype(jnp.int32)
        for c in range(len(CHUNKS))
    ]
    ids = (gate_index, up_index, down_index)
    weights = (gate_weight, up_weight, down_weight)
    blocks = gate_weight.shape[0]

    def pairs(c, second, by):
        found = []
        for z in range(4):
            for y in range(4):
                for t in range(8):
                    along_y = t % 2 == (1 if second else 0)
                    to = (z, (y + by) % 4) if along_y else ((z + by) % 4, y)
                    found.append(((z * 4 + y) * 8 + t, (to[0] * 4 + to[1]) * 8 + t))
        return found

    def send(c, up, down, second):
        axes = ("dp", "tensor")
        return (
            lax.ppermute(up, axes, pairs(c, second, 1)),
            lax.ppermute(down, axes, pairs(c, second, -1)),
        )

    starts = [sum(CHUNKS[:c]) for c in range(len(CHUNKS))]
    made, sent, grads = [], {}, None

    def chunk(c, *after):
        made.append(
            run_chunk(
                starts[c], CHUNKS[c], scale, ids, places[c], tokens, grad_out, weights,
                made[-1][5:] if made else None, after,
            )
        )

    def far(c, got, **order):
        return add_far(*got, *made[c][2:4], **order)

    def near(c, **order):
        sent[c] = add_near(made[c][4], *send(c, *sent[c], False), **order)

    def far2(c, **order):
        far_p, far_m, plus, minus, kept = sent[c]
        sent[c] = (*add_far2(*send(c, far_p, far_m, True), plus, minus, **order), kept)

    def last(c, grads):
        plus, minus, kept = sent[c]
        return add_last(starts[c], CHUNKS[c], blocks, kept, *send(c, plus, minus, True), grads)

    chunk(0)
    first = send(0, *made[0][:2], False)
    chunk(1)
    second = send(1, *made[1][:2], False)
    sent[0] = far(0, first, after=(made[1][0],))
    sent[1] = far(1, second, after=(sent[0][0],))
    partial, token = run_back(
        ids[:2], *made[1][5:], gate_weight, up_weight, width, (sent[0][0], sent[1][0])
    )
    summed = lax.psum_scatter(partial, "tensor", scatter_dimension=0, tiled=True)
    near(0, after=(token,), flops=LONG)
    far2(0)
    near(1, after=(sent[0][0],))
    grads = last(0, grads)
    far2(1)
    grads = last(1, grads)
    return (summed, *grads)


def solution(mesh):
    in_specs = (
        P("dp", None),
        P("dp", None),
        P("tensor", None, None, None),
        P("tensor", None, None, None),
        P("tensor", None, None, None),
        P("tensor", None),
        P("tensor", None),
        P("tensor", None),
    )
    out_specs = (
        P(("dp", "tensor"), None),
        P("tensor", "dp", None),
        P("tensor", "dp", None),
        P("tensor", "dp", None),
    )
    return jax.shard_map(body, mesh=mesh, in_specs=in_specs, out_specs=out_specs, check_vma=False)
```

```python
import functools
import math

import jax
import jax.numpy as jnp
from jax import lax
from jax.experimental import pallas as pl
from jax.experimental.pallas import tpu as pltpu
from jax.sharding import PartitionSpec as P

BLK = 128
ROWS = 96
SET = 3 * ROWS
NNZ = 12
BF = jnp.bfloat16
F32 = jnp.float32
CHUNKS = (7,5)
VMEM_BYTES = 53 << 20
FULL_BYTES = (64 << 20) - (64 << 10)
LONG = 200 * 10**9


def dot(a, b):
    return jnp.dot(a, b, preferred_element_type=F32)


def dot_nt(a, b):
    return lax.dot_general(a, b, (((1,), (1,)), ((), ())), preferred_element_type=F32)


def block_at(ref, block):
    return ref[:, pl.ds(pl.multiple_of(block * BLK, BLK), BLK)]


def chunk_kernel(
    first, scale,
    gate_ids, up_ids, down_ids, place,
    tok, out_grad, w_gate, w_up, w_down, *rest,
):
    far_p, far_m, plus, minus, own, gate_out, up_out, terms = rest[-8:]
    step = pl.program_id(0)
    j = first + step
    y, z, flip = place[0], place[1], place[2]

    def forward(source, ids, weight, transposed):
        half = source.shape[0] // 2
        return jnp.concatenate(
            [forward_rows(source, ids, weight, transposed, r, half) for r in (0, half)], axis=0
        )

    def forward_rows(source, ids, weight, transposed, row, rows):
        total = None
        for k in range(0, NNZ, 2):
            left = jnp.concatenate(
                [block_at(source, ids[j, k + i])[row : row + rows] for i in range(2)], axis=1
            )
            if transposed:
                right = jnp.concatenate([weight[0, k], weight[0, k + 1]], axis=1)
                part = dot_nt(left, right)
            else:
                part = dot(left, weight[0, k : k + 2].reshape(2 * BLK, BLK))
            total = part if total is None else total + part
        return total

    gate_lin = forward(tok, gate_ids, w_gate, False)
    up_lin = forward(tok, up_ids, w_up, False)

    hidden_grad = forward(out_grad, down_ids, w_down, True)
    sigmoid = jax.nn.sigmoid(gate_lin)
    activated = gate_lin * sigmoid
    hidden = (activated * up_lin).astype(BF)
    up_grad = (hidden_grad * activated).astype(BF)
    gate_grad = (
        hidden_grad * up_lin * sigmoid * (1.0 + gate_lin * (1.0 - sigmoid))
    ).astype(BF)
    gate_out[...] = gate_grad
    up_out[...] = up_grad
    hidden_t, gate_t, up_t = hidden.T, gate_grad.T, up_grad.T

    def put(z_rel, w, term):
        for shard in range(4):
            y_rel = lax.rem(shard - y + 4, 4)
            at = jnp.where(flip == 0, y_rel * 4 + z_rel, z_rel * 4 + y_rel)
            terms[at, w * ROWS : (w + 1) * ROWS] = term[shard * ROWS : (shard + 1) * ROWS]

    cut = 2 * BLK
    for z_first in (0, 2):
        groups = [3 * lax.rem(z + z_first + n, 4) for n in range(2)]
        for w, (left, source, ids) in enumerate(
            ((gate_t, tok, gate_ids), (up_t, tok, up_ids), (hidden_t, out_grad, down_ids))
        ):
            right = jnp.concatenate(
                [block_at(source, ids[j, g + i]) for g in groups for i in range(3)], axis=1
            )
            wide = dot(left[:, :cut], right[:cut]) + dot(left[:, cut:], right[cut:])
            wide = (wide * scale).astype(BF)
            for n in range(2):
                parts = [wide[:, i * BLK : (i + 1) * BLK] for i in range(3 * n, 3 * n + 3)]
                parts = parts if w == 2 else [p.T for p in parts]
                put(z_first + n, w, jnp.concatenate(parts, axis=0))

    own[...] = terms[0:4]
    plus[...] = terms[4:8]
    far_p[...] = terms[8:10]
    far_m[...] = terms[10:12]
    minus[...] = terms[12:16]


def run_chunk(first, size, scale, ids, place, tok, out_grad, weights, grads, after):
    tokens = tok.shape[0]
    hbm = pl.BlockSpec(memory_space=pl.ANY)
    vmem = pl.BlockSpec(memory_space=pltpu.VMEM)
    weight = pl.BlockSpec((1, NNZ, BLK, BLK), lambda i, *_: (first + i, 0, 0, 0))
    hidden = pl.BlockSpec((tokens, BLK), lambda i, *_: (0, first + i))
    extra = [*(grads or ()), *after]

    def terms_of(n):
        return pl.BlockSpec((n, SET, BLK), lambda i, *_: (0, i, 0)), jax.ShapeDtypeStruct(
            (n, size * SET, BLK), BF
        )

    far, direct = terms_of(2), terms_of(4)
    grad_shape = jax.ShapeDtypeStruct((tokens, weights[0].shape[0] * BLK), BF)
    return pl.pallas_call(
        functools.partial(chunk_kernel, first, scale),
        grid_spec=pltpu.PrefetchScalarGridSpec(
            num_scalar_prefetch=4,
            grid=(size,),
            in_specs=[vmem] * 2 + [weight] * 3 + [hbm] * len(extra),
            out_specs=[far[0]] * 2 + [direct[0]] * 3 + [hidden] * 2,
            scratch_shapes=[pltpu.VMEM((16, SET, BLK), BF)],
        ),
        out_shape=[far[1]] * 2 + [direct[1]] * 3 + [grad_shape] * 2,
        input_output_aliases={9: 5, 10: 6} if grads else {},
        compiler_params=pltpu.CompilerParams(vmem_limit_bytes=VMEM_BYTES),
        cost_estimate=pl.CostEstimate(
            flops=25 * 10**9, bytes_accessed=20 << 20, transcendentals=0
        ),
        name="chunk",
    )(*ids, place, tok, out_grad, *weights, *extra)


def back_kernel(gate_ids, up_ids, gate_grad, up_grad, w_gate, w_up, out, token, total, piece, sem):
    j = pl.program_id(0)
    rows, width = total.shape

    @pl.when(j == 0)
    def _():
        total[...] = jnp.zeros_like(total)
        token[...] = jnp.zeros_like(token)

    for ids, grad, weight in ((gate_ids, gate_grad, w_gate), (up_ids, up_grad, w_up)):
        for k in range(0, NNZ, 2):
            right = weight[0, k : k + 2].reshape(2 * BLK, BLK)
            part = jnp.concatenate(
                [dot_nt(grad[r : r + rows // 2], right) for r in (0, rows // 2)], axis=0
            )
            for i in range(2):
                at = pl.ds(pl.multiple_of(ids[j, k + i] * BLK, BLK), BLK)
                total[:, at] = total[:, at] + part[:, i * BLK : (i + 1) * BLK]

    @pl.when(j == pl.num_programs(0) - 1)
    def _():
        count = 4
        step = width // count
        copies = []
        for q in range(count):
            at = pl.ds(q * step, step)
            piece[q] = total[:, at].astype(BF)
            copies.append(pltpu.make_async_copy(piece.at[q], out.at[:, at], sem.at[q]))
            copies[-1].start()
        for copy in copies:
            copy.wait()


def run_back(ids, gate_grad, up_grad, w_gate, w_up, width, after):
    tokens = gate_grad.shape[0]
    blocks = w_gate.shape[0]
    hidden = pl.BlockSpec((tokens, BLK), lambda i, *_: (0, i))
    weight = pl.BlockSpec((1, NNZ, BLK, BLK), lambda i, *_: (i, 0, 0, 0))
    hbm = pl.BlockSpec(memory_space=pl.ANY)

    def kernel(*refs):
        back_kernel(*refs[:6], *refs[6 + len(after) :])

    return pl.pallas_call(
        kernel,
        grid_spec=pltpu.PrefetchScalarGridSpec(
            num_scalar_prefetch=2,
            grid=(blocks,),
            in_specs=[hidden, hidden, weight, weight] + [hbm] * len(after),
            out_specs=[hbm, pl.BlockSpec((8, BLK), lambda i, *_: (0, 0))],
            scratch_shapes=[
                pltpu.VMEM((tokens, width), F32),
                pltpu.VMEM((4, tokens, width // 4), BF),
                pltpu.SemaphoreType.DMA((4,)),
            ],
        ),
        out_shape=[
            jax.ShapeDtypeStruct((tokens, width), BF),
            jax.ShapeDtypeStruct((8, BLK), F32),
        ],
        compiler_params=pltpu.CompilerParams(vmem_limit_bytes=FULL_BYTES),
        cost_estimate=pl.CostEstimate(
            flops=25 * 10**9, bytes_accessed=16 << 20, transcendentals=0
        ),
        name="back",
    )(*ids, gate_grad, up_grad, w_gate, w_up, *after)


def wide(a):
    return a[...].astype(F32)


def call(kernel, name, grid, in_specs, out_specs, out_shape, args, aliases=None, after=(), room=False, flops=0):
    taken = len(args)

    def run(*refs):
        kernel(*refs[:taken], *refs[taken + len(after) :])

    return pl.pallas_call(
        run,
        grid=grid,
        in_specs=in_specs + [pl.BlockSpec(memory_space=pl.ANY)] * len(after),
        out_specs=out_specs,
        out_shape=out_shape,
        input_output_aliases=aliases or {},
        compiler_params=pltpu.CompilerParams(vmem_limit_bytes=VMEM_BYTES if room else FULL_BYTES),
        cost_estimate=pl.CostEstimate(flops=flops, bytes_accessed=0, transcendentals=0),
        name=name,
    )(*args, *after)


def far_kernel(far_p, far_m, plus, minus, plus_out, minus_out):
    plus_out[...] = (wide(plus) + wide(far_p)).astype(BF)
    minus_out[...] = (wide(minus) + wide(far_m)).astype(BF)


def add_far(far_p, far_m, plus, minus, **order):
    rows = plus.shape[1]
    one = (1, rows, BLK)
    low = pl.BlockSpec(one, lambda i: (i, 0, 0))
    high = pl.BlockSpec(one, lambda i: (i + 2, 0, 0))
    shape = jax.ShapeDtypeStruct(plus.shape, BF)
    return call(
        far_kernel, "add_far", (2,), [low, low, low, high], [low, high], [shape, shape],
        (far_p, far_m, plus, minus), {2: 0, 3: 1}, **order,
    )


def near_kernel(own, got_p, got_m, far_p, far_m, plus, minus, kept):
    total = (wide(own) + wide(got_p) + wide(got_m)).astype(BF)
    kept[...] = total[0]
    plus[...] = total[1]
    minus[...] = total[3]

    @pl.when(pl.program_id(0) == 0)
    def _():
        far_p[...] = total[2]

    @pl.when(pl.program_id(0) == 1)
    def _():
        far_m[...] = total[2]


def add_near(own, got_p, got_m, **order):
    half = own.shape[1] // 2
    block = pl.BlockSpec((4, half, BLK), lambda i: (0, i, 0))
    part = pl.BlockSpec((half, BLK), lambda i: (i, 0))
    fixed = pl.BlockSpec((half, BLK), lambda i: (0, 0))
    small = jax.ShapeDtypeStruct((half, BLK), BF)
    large = jax.ShapeDtypeStruct((2 * half, BLK), BF)
    return call(
        near_kernel, "add_near", (2,), [block] * 3, [fixed] * 2 + [part] * 3,
        [small] * 2 + [large] * 3, (own, got_p, got_m), **order,
    )


def add_far2(far_p, far_m, plus, minus, **order):
    half = far_p.shape[0]
    whole = pl.BlockSpec((half, BLK), lambda i: (0, 0))
    high = pl.BlockSpec((half, BLK), lambda i: (1, 0))
    shape = jax.ShapeDtypeStruct(plus.shape, BF)
    return call(
        far_kernel, "add_far2", (1,), [whole, whole, whole, high], [whole, high], [shape, shape],
        (far_p, far_m, plus, minus), {2: 0, 3: 1}, **order,
    )


def last_kernel(first, size, kept, got_p, got_m, *refs):
    outs, total, sem = refs[-5:-2], refs[-2], refs[-1]
    sums = wide(kept) + wide(got_p) + wide(got_m)
    copies = []
    for w in range(3):
        for i in range(size):
            total[w, i] = sums[i * SET + w * ROWS : i * SET + (w + 1) * ROWS]
        to = outs[w].at[pl.ds(first, size)]
        copies.append(pltpu.make_async_copy(total.at[w], to, sem.at[w]))
        copies[-1].start()
    for copy in copies:
        copy.wait()


def add_last(first, size, blocks, kept, got_p, got_m, grads):
    whole = pl.BlockSpec(kept.shape, lambda i: (0, 0))
    hbm = pl.BlockSpec(memory_space=pl.ANY)
    given = [] if grads is None else list(grads)
    return pl.pallas_call(
        functools.partial(last_kernel, first, size),
        grid=(1,),
        in_specs=[whole] * 3 + [hbm] * len(given),
        out_specs=[hbm] * 3,
        out_shape=[jax.ShapeDtypeStruct((blocks, ROWS, BLK), F32)] * 3,
        scratch_shapes=[
            pltpu.VMEM((3, size, ROWS, BLK), F32),
            pltpu.SemaphoreType.DMA((3,)),
        ],
        input_output_aliases={3 + i: i for i in range(len(given))},
        compiler_params=pltpu.CompilerParams(vmem_limit_bytes=FULL_BYTES),
        cost_estimate=pl.CostEstimate(flops=0, bytes_accessed=0, transcendentals=0),
        name="add_last",
    )(kept, got_p, got_m, *given)


def body(tokens, grad_out, gate_weight, up_weight, down_weight, gate_index, up_index, down_index):
    row_count, width = tokens.shape
    scale = 1.0 / math.sqrt(row_count * lax.axis_size("dp"))
    me, flip = lax.axis_index("dp"), lax.rem(lax.axis_index("tensor"), 2)
    places = [
        jnp.stack([lax.rem(me, 4), lax.div(me, 4), flip]).astype(jnp.int32)
        for c in range(len(CHUNKS))
    ]
    ids = (gate_index, up_index, down_index)
    weights = (gate_weight, up_weight, down_weight)
    blocks = gate_weight.shape[0]

    def pairs(c, second, by):
        found = []
        for z in range(4):
            for y in range(4):
                for t in range(8):
                    along_y = t % 2 == (1 if second else 0)
                    to = (z, (y + by) % 4) if along_y else ((z + by) % 4, y)
                    found.append(((z * 4 + y) * 8 + t, (to[0] * 4 + to[1]) * 8 + t))
        return found

    def send(c, up, down, second):
        axes = ("dp", "tensor")
        return (
            lax.ppermute(up, axes, pairs(c, second, 1)),
            lax.ppermute(down, axes, pairs(c, second, -1)),
        )

    starts = [sum(CHUNKS[:c]) for c in range(len(CHUNKS))]
    made, sent, grads = [], {}, None

    def chunk(c, *after):
        made.append(
            run_chunk(
                starts[c], CHUNKS[c], scale, ids, places[c], tokens, grad_out, weights,
                made[-1][5:] if made else None, after,
            )
        )

    def far(c, got, **order):
        return add_far(*got, *made[c][2:4], **order)

    def near(c, **order):
        sent[c] = add_near(made[c][4], *send(c, *sent[c], False), **order)

    def far2(c, **order):
        far_p, far_m, plus, minus, kept = sent[c]
        sent[c] = (*add_far2(*send(c, far_p, far_m, True), plus, minus, **order), kept)

    def last(c, grads):
        plus, minus, kept = sent[c]
        return add_last(starts[c], CHUNKS[c], blocks, kept, *send(c, plus, minus, True), grads)

    chunk(0)
    first = send(0, *made[0][:2], False)
    chunk(1)
    second = send(1, *made[1][:2], False)
    sent[0] = far(0, first, after=(made[1][0],))
    sent[1] = far(1, second, after=(sent[0][0],))
    partial, token = run_back(
        ids[:2], *made[1][5:], gate_weight, up_weight, width, (sent[0][0], sent[1][0])
    )
    summed = lax.psum_scatter(partial, "tensor", scatter_dimension=0, tiled=True)
    near(0, after=(token,), flops=LONG)
    far2(0)
    near(1, after=(sent[0][0],))
    grads = last(0, grads)
    far2(1)
    grads = last(1, grads)
    return (summed, *grads)


def solution(mesh):
    in_specs = (
        P("dp", None),
        P("dp", None),
        P("tensor", None, None, None),
        P("tensor", None, None, None),
        P("tensor", None, None, None),
        P("tensor", None),
        P("tensor", None),
        P("tensor", None),
    )
    out_specs = (
        P(("dp", "tensor"), None),
        P("tensor", "dp", None),
        P("tensor", "dp", None),
        P("tensor", "dp", None),
    )
    return jax.shard_map(body, mesh=mesh, in_specs=in_specs, out_specs=out_specs, check_vma=False)
```
